512 devices in a mesh: frame: 32 (over z, y_lo, core), row: 16 (over y_hi, x).
Axes of the slice: x: 4, y: 8 (y_hi: 4, y_lo: 2; y = y_hi * 2 + y_lo), z: 8, core: 2. Of those that a mesh axis runs over, the one named last changes fastest.
Arguments:
- queries: bfloat16 [32, 2048, 2560], P('frame', 'row'), may hold values from -12 to 12
- key_states: bfloat16 [32, 2048, 2560], P('frame', 'row'), may hold values from -12 to 12
- value_states: bfloat16 [32, 2048, 2560], P('frame', 'row'), may hold values from -6 to 6
- radial_mask: int32 [5, 32, 5], replicated, may hold values from 0 to 1, as said below
Outputs:
- attended: bfloat16 [32, 2048, 2560], P('frame', 'row')
The draws below stay inside these ranges and needn't reach their ends.
Inputs may be any that keep to these rules, and one draw needn't show every extreme that they name: radial_mask[e, b, j] is 1 only where |e - 2| + |j - 2| <= 2, and radial_mask[2, b, 2] is 1 for every block b.
All inputs are finite; a program needn't handle non-finite values.
Results may differ from the reference program's by a relative error of at most 0.0054.
Values may be sent and summed in bfloat16 or wider, within the bound.
No kernel may reach another device: no remote copies, remote signals or barrier semaphores. Data moves between devices by JAX's collectives and lax.ppermute only.
A program may use at most 64 MiB of HBM per device.

```python
from functools import partial
import jax
import jax.numpy as jnp
from jax import lax

HDIM = 128
BLK = 64
REACH = 2
WIDTH = 2560
NBLK = 32
ROWS = 2048
FRAMES = 32


def loguniform_scales(source_key, shape_rows, lowest, highest):
    return jnp.exp(jax.random.uniform(source_key, shape_rows, jnp.float32, jnp.log(lowest), jnp.log(highest)))


def draw_queries(key, part):
    key = jax.random.fold_in(key, 11)
    noise_key, scale_key = jax.random.split(key)
    noise_draw = jax.random.normal(noise_key, (FRAMES, ROWS, WIDTH), jnp.float32)
    result = noise_draw * 0.7 * loguniform_scales(scale_key, (FRAMES, ROWS, 1), 0.3, 3.0)
    return jnp.clip(result, -12.0, 12.0).astype(jnp.bfloat16)


def draw_key_states(key, part):
    key = jax.random.fold_in(key, 12)
    noise_key, scale_key = jax.random.split(key, 2)
    noise_draw = jax.random.normal(noise_key, (FRAMES, ROWS, WIDTH), jnp.float32)
    result = noise_draw * 0.7 * loguniform_scales(scale_key, (FRAMES, ROWS, 1), 0.3, 3.0)
    return jnp.clip(result, -12.0, 12.0).astype(jnp.bfloat16)


def draw_radial_mask(key, part):
    key = jax.random.fold_in(key, 13)
    level_key, pick_key = jax.random.split(key)
    offset_count = 2 * REACH + 1
    density = jax.random.randint(level_key, (1, NBLK, 1), 2, 10)
    picks = jax.random.randint(pick_key, (offset_count, NBLK, offset_count), 0, 10)
    frame_steps = jnp.abs(jnp.arange(offset_count) - REACH)[:, None, None]
    row_steps = jnp.abs(jnp.arange(offset_count) - REACH)[None, None, :]
    inside = frame_steps + row_steps <= REACH
    centre = (frame_steps == 0) & (row_steps == 0)
    return jnp.where(centre | inside & (picks < density), 1, 0).astype(jnp.int32)


def steps_of(own_key, dims, cuts, low, high):
    def one(position, shards_of):
        heights = jax.random.uniform(jax.random.fold_in(jax.random.fold_in(own_key, 6), position), (shards_of,), jnp.float32, low / len(cuts), high / len(cuts))
        return jnp.repeat(jnp.exp(heights), dims[position] // shards_of).reshape((-1,) + (1,) * (len(dims) - position - 1))

    loudness = one(*cuts[0])
    for cut in cuts[1:]:
        loudness = loudness * one(*cut)
    return loudness


def normal_values(own_key, extent, width, reach, shards=(), kind=jnp.bfloat16):
    values = jax.random.normal(own_key, extent, jnp.float32) * width
    if len(shards) > 0:
        values = steps_of(own_key, extent, shards, -0.22, 0.18) * values
    return jnp.clip(values, min=-reach, max=reach).astype(kind)


def setup_inputs(seed: int = 0) -> dict:
    seeds = jax.random.split(jax.random.key(seed), 5)
    return {
        "queries": draw_queries(jax.random.fold_in(seeds[4], 71), 0),
        "key_states": draw_key_states(jax.random.fold_in(seeds[4], 71), 0),
        "value_states": normal_values(seeds[2], (FRAMES, ROWS, WIDTH), 1.0, 6.0, ((0, 32), (1, 16))),
        "radial_mask": draw_radial_mask(jax.random.fold_in(seeds[4], 71), 0),
    }


def attend_block(frame_at, block_at, queries, keys_padded, values_padded, radial_mask):
    frame_total, row_total, width_total = queries.shape
    block_total = row_total // BLK
    offset_count = 2 * REACH + 1
    head_count = width_total // HDIM
    zero_index = jnp.zeros((), jnp.int32)
    query_heads = lax.dynamic_slice(queries, (frame_at, block_at * BLK, zero_index), (1, BLK, width_total))
    query_heads = query_heads.reshape(BLK, head_count, HDIM).astype(jnp.float32)
    key_parts = []
    value_parts = []
    for frame_step in range(offset_count):
        start_index = (frame_at + frame_step, block_at * BLK, zero_index)
        key_parts.append(lax.dynamic_slice(keys_padded, start_index, (1, offset_count * BLK, width_total)))
        value_parts.append(lax.dynamic_slice(values_padded, start_index, (1, offset_count * BLK, width_total)))
    window_keys = jnp.concatenate(key_parts, axis=0).reshape(-1, head_count, HDIM).astype(jnp.float32)
    window_values = jnp.concatenate(value_parts, axis=0).reshape(-1, head_count, HDIM).astype(jnp.float32)
    offsets = jnp.arange(offset_count, dtype=jnp.int32) - REACH
    frames_valid = (frame_at + offsets >= 0) & (frame_at + offsets < frame_total)
    blocks_valid = (block_at + offsets >= 0) & (block_at + offsets < block_total)
    mask_rows = lax.dynamic_index_in_dim(radial_mask, block_at, axis=1, keepdims=False)
    allowed = (mask_rows > 0) & frames_valid[:, None] & blocks_valid[None, :]
    allowed_keys = jnp.broadcast_to(allowed[:, :, None], (offset_count, offset_count, BLK)).reshape(-1)
    scores = jnp.einsum("qhd,khd->hqk", query_heads, window_keys) * HDIM ** -0.5
    scores = jnp.where(allowed_keys[None, None, :], scores, -jnp.inf)
    weights = jnp.exp(scores - jnp.max(scores, axis=2, keepdims=True))
    weight_sum = jnp.sum(weights, axis=2)
    rounded_weights = lax.optimization_barrier(weights.astype(jnp.bfloat16)).astype(jnp.float32)
    attended_block = jnp.einsum("hqk,khd->qhd", rounded_weights, window_values) / jnp.transpose(weight_sum)[:, :, None]
    return attended_block.reshape(BLK, width_total).astype(jnp.bfloat16)


def reference(queries, key_states, value_states, radial_mask):
    frame_total, row_total, width_total = queries.shape
    margin = REACH * BLK
    padding = ((REACH, REACH), (margin, margin), (0, 0))
    keys_padded = jnp.pad(key_states, padding)
    values_padded = jnp.pad(value_states, padding)

    def one_frame(frame_at):
        per_block = partial(attend_block, frame_at, queries=queries, keys_padded=keys_padded, values_padded=values_padded, radial_mask=radial_mask)
        blocks = lax.map(per_block, jnp.arange(row_total // BLK, dtype=jnp.int32))
        return blocks.reshape(row_total, width_total)

    return lax.map(one_frame, jnp.arange(frame_total, dtype=jnp.int32))
```

```python
import functools

import jax
import jax.numpy as jnp
import numpy as np
from jax import lax
from jax.experimental import pallas as pl
from jax.experimental.pallas import tpu as pltpu
from jax.sharding import PartitionSpec as P

HDIM = 128
BLK = 64
REACH = 2
NEG = -1e30
SCALE = HDIM ** -0.5 * 1.4426950408889634
AXES = ("frame", "row")
GROUP = 4
XN = 4
VMEM = pl.BlockSpec(memory_space=pltpu.VMEM)
SMEM = pl.BlockSpec(memory_space=pltpu.SMEM)
ANY = pl.BlockSpec(memory_space=pl.ANY)
FRAME_STEPS = (-2, -1, 0, 1, 2)
HALO_STEPS = (-1, 0, 1)
OWN_KEYS = 2 * BLK * len(FRAME_STEPS)


def pairs_of(frames, rows, target):
    pairs = []
    for frame in range(frames):
        for row in range(rows):
            to = target(frame, row)
            if to is not None and 0 <= to[0] < frames and 0 <= to[1] < rows:
                pairs.append((frame * rows + row, to[0] * rows + to[1]))
    return pairs


def key_block_table():
    own = [(step, block) for step in FRAME_STEPS for block in (0, 1)]
    halo = []
    for step in HALO_STEPS:
        reach = REACH - abs(step)
        halo += [(step, block) for block in range(-reach, 0)]
        halo += [(step, block) for block in range(2, 2 + reach)]
    return own + halo


def bias_of(radial_mask, frame_first, row_at, frame_total):
    table = key_block_table()
    offsets = 2 * REACH + 1
    pick = np.zeros((2, len(table), offsets * 2 * offsets), np.float32)
    for query in range(2):
        for at, (step, block) in enumerate(table):
            offset = block - query + REACH
            if 0 <= offset < offsets:
                pick[query, at, ((step + REACH) * 2 + query) * offsets + offset] = 1.0
    rows = lax.dynamic_slice_in_dim(radial_mask, row_at * 2, 2, 1)
    chosen = jnp.sum(jnp.asarray(pick) * rows.reshape(1, 1, -1).astype(jnp.float32), axis=2)
    steps = jnp.asarray(np.array([s for s, _ in table], np.int32))
    blocks = jnp.asarray(np.array([b for _, b in table], np.int32)) + row_at * 2
    inside = (blocks >= 0) & (blocks < radial_mask.shape[1])
    frames = frame_first + jnp.arange(GROUP, dtype=jnp.int32)[:, None] + steps[None, :]
    valid = (frames >= 0) & (frames < frame_total) & inside[None, :]
    allowed = (chosen[None] > 0) & valid[:, None, :]
    bias = jnp.where(allowed, 0.0, NEG).astype(jnp.float32)
    return jnp.repeat(bias, BLK, axis=2)


def pack_kernel(at_ref, q_ref, k_ref, v_ref, out0, out1, out2, out3, sems):
    me = at_ref[0]
    outs = (out0, out1, out2, out3)
    width = out0.shape[2]
    copies = []
    for slot in (1, 2, 3, 0):
        columns = pl.ds(pl.multiple_of((me ^ slot) * width, HDIM), width)
        for which, source in enumerate((k_ref, v_ref, q_ref)):
            copies.append(
                pltpu.make_async_copy(
                    source.at[:, columns], outs[slot].at[which], sems.at[slot, which]
                )
            )
    for copy in copies:
        copy.start()
    for copy in copies:
        copy.wait()


def unpack_kernel(in_ref, out_ref, sems):
    width = in_ref.shape[2]
    copies = [
        pltpu.make_async_copy(
            in_ref.at[part], out_ref.at[:, pl.ds(part * width, width)], sems.at[part]
        )
        for part in range(GROUP)
    ]
    for copy in copies:
        copy.start()
    for copy in copies:
        copy.wait()


def corner_kernel(own_pair, at_ref, *refs):
    me, x_at = at_ref[0], at_ref[1]
    out, sems = refs[-2], refs[-1]
    lows, highs = refs[: (len(refs) - 2) // 2], refs[(len(refs) - 2) // 2 : -2]
    length = lows[0].shape[2]
    if own_pair:
        slot = jnp.where(me < 2, me, 3 - me)
    else:
        slot = jnp.where(me < 2, 1 - me, me - 2)

    def from_low(source):
        rows = pl.ds(length - BLK, BLK)
        return pltpu.make_async_copy(source.at[slot, :, rows], out.at[:, pl.ds(0, BLK)], sems.at[0])

    def from_high(source):
        rows = pl.ds(0, BLK)
        return pltpu.make_async_copy(source.at[slot, :, rows], out.at[:, pl.ds(BLK, BLK)], sems.at[1])

    if own_pair:

        @pl.when(x_at == 0)
        def _():
            from_low(lows[1]).start()

        @pl.when(x_at != 0)
        def _():
            from_low(lows[0]).start()

        @pl.when(x_at == XN - 1)
        def _():
            from_high(highs[1]).start()

        @pl.when(x_at != XN - 1)
        def _():
            from_high(highs[0]).start()

    else:
        from_low(lows[0]).start()
        from_high(highs[0]).start()
    from_low(lows[0]).wait()
    from_high(highs[0]).wait()


def corner(own_pair, place, lows, highs):
    shape = lows[0].shape
    return pl.pallas_call(
        functools.partial(corner_kernel, own_pair),
        in_specs=[SMEM] + [ANY] * (len(lows) + len(highs)),
        out_specs=VMEM,
        out_shape=jax.ShapeDtypeStruct((2, 2 * BLK, shape[3]), jnp.bfloat16),
        scratch_shapes=[pltpu.SemaphoreType.DMA((2,))],
        compiler_params=pltpu.CompilerParams(vmem_limit_bytes=4 * 2**20),
    )(place, *lows, *highs)


def head_scores(query, keys, bias):
    scores = jnp.concatenate(
        [
            lax.dot_general(query, k, (((1,), (1,)), ((), ())), preferred_element_type=jnp.float32)
            for k in keys
        ],
        axis=1,
    )
    return jnp.concatenate([scores[:BLK] + bias[0:1], scores[BLK:] + bias[1:2]], axis=0)


def weighted(weights, values):
    rounded = weights.astype(jnp.bfloat16)
    start, out = 0, 0
    for v in values:
        out = out + jnp.dot(
            rounded[:, start : start + v.shape[0]], v, preferred_element_type=jnp.float32
        )
        start += v.shape[0]
    return out


def own_kernel(
    at_ref, bias_ref, got0, got1, got2, got3, own, oth, z_own, z_oth,
    out_ref, top_ref, sum_ref, keys, values, queries,
):
    me = at_ref[0]
    upper = me >= 2

    def one_head(head, carry):
        lanes = pl.ds(pl.multiple_of(head * HDIM, HDIM), HDIM)
        for slot, got in enumerate((got0, got1, got2, got3)):
            queries[me ^ slot] = got[2, :, lanes]
        for which, store in ((0, keys), (1, values)):
            for slot in range(2):
                store[2 + (me ^ slot)] = own[slot, which, :, lanes]
                store[2 + (me ^ slot ^ 2)] = oth[slot, which, :, lanes]
                at = jnp.where(upper, (me ^ slot) - 2, 6 + (me ^ slot))
                store[at] = z_own[slot, which, :, lanes]
                at = jnp.where(upper, 6 + (me ^ slot ^ 2), (me ^ slot ^ 2) - 2)
                store[at] = z_oth[slot, which, :, lanes]
        for frame in range(GROUP):
            near = [frame + 2 + step for step in FRAME_STEPS]
            scores = head_scores(
                queries[frame], [keys[at] for at in near], bias_ref[frame, :, :OWN_KEYS]
            )
            top = jnp.max(scores, axis=1, keepdims=True)
            weights = jnp.exp2((scores - top) * SCALE)
            total = jnp.sum(weights, axis=1, keepdims=True)
            out_ref[frame, :, lanes] = weighted(weights, [values[at] for at in near])
            top_ref[frame, :, lanes] = jnp.broadcast_to(top, (top.shape[0], HDIM))
            sum_ref[frame, :, lanes] = jnp.broadcast_to(total, (top.shape[0], HDIM))
        return carry

    lax.fori_loop(0, own.shape[3] // HDIM, one_head, 0)


def halo_kernel(
    frames, at_ref, bias_ref, got0, got1, got2, got3, sofar, top_in, sum_in,
    low_own, low_own2, low_oth, high_own, high_own2, high_oth, *rest
):
    corners, (out_ref, keys, values, queries) = rest[:-4], rest[-4:]
    me, x_at = at_ref[0], at_ref[1]
    upper = me >= 2
    length = low_own.shape[2]

    def one_head(head, carry):
        lanes = pl.ds(pl.multiple_of(head * HDIM, HDIM), HDIM)
        below, above = slice(0, length), slice(length, 2 * length)
        for slot, got in enumerate((got0, got1, got2, got3)):
            queries[me ^ slot] = got[2, :, lanes]
        for which, store in ((0, keys), (1, values)):
            for slot in range(2):
                at = 1 + (me ^ slot)
                store[at, below] = jnp.where(
                    x_at == 0, low_own2[slot, which, :, lanes], low_own[slot, which, :, lanes]
                )
                store[at, above] = jnp.where(
                    x_at == XN - 1, high_own2[slot, which, :, lanes], high_own[slot, which, :, lanes]
                )
                at = 1 + (me ^ slot ^ 2)
                store[at, below] = low_oth[slot, which, :, lanes]
                store[at, above] = high_oth[slot, which, :, lanes]
            for arrived, at in zip(corners, (jnp.where(upper, 0, 5), jnp.where(upper, 5, 0))):
                store[at, length - BLK : length + BLK] = arrived[which, :, lanes]
        for at_out, frame in enumerate(frames):
            spans = []
            for step in HALO_STEPS:
                reach = (REACH - abs(step)) * BLK
                spans.append((frame + 1 + step, slice(length - reach, length + reach)))
            scores = head_scores(
                queries[frame], [keys[at, span] for at, span in spans], bias_ref[frame, :, OWN_KEYS:]
            )
            top_own = top_in[frame, :, lanes]
            top = jnp.maximum(top_own, jnp.max(scores, axis=1, keepdims=True))
            again = jnp.exp2((top_own - top) * SCALE)
            weights = jnp.exp2((scores - top[:, 0:1]) * SCALE)
            total = sum_in[frame, :, lanes] * again + jnp.sum(weights, axis=1, keepdims=True)
            out = sofar[frame, :, lanes] * again + weighted(
                weights, [values[at, span] for at, span in spans]
            )
            out_ref[at_out, :, lanes] = (out / total).astype(jnp.bfloat16)
        return carry

    lax.fori_loop(0, low_own.shape[3] // HDIM, one_head, 0)


def attend(kernel, out_shape, scratch, work, place, bias, arrays):
    length, width = arrays[0].shape[1:]
    return pl.pallas_call(
        kernel,
        in_specs=[SMEM] + [VMEM] * (1 + len(arrays)),
        out_specs=jax.tree.map(lambda _: VMEM, out_shape),
        out_shape=out_shape,
        scratch_shapes=[pltpu.VMEM(scratch, jnp.bfloat16)] * 2
        + [pltpu.VMEM((GROUP, length, HDIM), jnp.bfloat16)],
        compiler_params=pltpu.CompilerParams(vmem_limit_bytes=16 * 2**20),
        cost_estimate=pl.CostEstimate(
            flops=4 * work * width * length, bytes_accessed=8_000_000,
            transcendentals=work * width * length // HDIM,
        ),
    )(place, bias, *arrays)


def shards(frame_total, row_total, queries, key_states, value_states, radial_mask):
    length, width = queries.shape[1:]
    part = width // GROUP
    frame_at = lax.axis_index("frame")
    row_at = lax.axis_index("row")
    me = frame_at % GROUP
    x_at = row_at % XN
    place = jnp.stack([me, x_at]).astype(jnp.int32)

    def send(array, target):
        return lax.ppermute(array, AXES, pairs_of(frame_total, row_total, target))

    packed = pl.pallas_call(
        pack_kernel,
        in_specs=[SMEM] + [ANY] * 3,
        out_specs=[VMEM] * GROUP,
        out_shape=[jax.ShapeDtypeStruct((3, length, part), jnp.bfloat16)] * GROUP,
        scratch_shapes=[pltpu.SemaphoreType.DMA((GROUP, 3))],
        compiler_params=pltpu.CompilerParams(vmem_limit_bytes=56 * 2**20),
    )(place, queries[0], key_states[0], value_states[0])

    def flip(bits):
        return lambda f, r: (f ^ bits, r)

    groups = [list(range(f, f + GROUP)) for f in range(0, frame_total, GROUP)]
    arrived = [packed[0]] + [send(packed[s], flip(s)) for s in range(1, GROUP)]
    own = jnp.stack([arrived[0][:2], arrived[1][:2]])
    oth = jnp.stack([arrived[2][:2], arrived[3][:2]])

    def row_first(by):
        edge = XN - 1 if by > 0 else 0
        return lambda f, r: (f, r + by) if r % XN != edge else (f, r - by * (XN - 1))

    def row_second(by):
        edge = 0 if by > 0 else XN - 1
        return lambda f, r: (f, r + by * XN) if r % XN == edge else None

    def row_direct(by):
        return lambda f, r: (f, r + by)

    def z_target(own_pair):
        def target(f, r):
            up = (f % GROUP >= 2) == own_pair
            return (f + GROUP if up else f - GROUP, r)

        return target

    low_own, high_own = send(own, row_first(1)), send(own, row_first(-1))
    z_own = send(own, z_target(True))
    low_own2, high_own2 = send(low_own, row_second(1)), send(high_own, row_second(-1))
    low_oth, high_oth = send(oth, row_direct(1)), send(oth, row_direct(-1))
    later, z_own, low_own, high_own = lax.optimization_barrier((oth, z_own, low_own, high_own))
    z_oth = send(later, z_target(False))
    bias = bias_of(radial_mask, frame_at - me, row_at, frame_total)
    sums = [jax.ShapeDtypeStruct((GROUP, length, part), jnp.float32)] * 3
    partial = attend(
        own_kernel, sums, (GROUP + 4, length, HDIM), GROUP * OWN_KEYS, place, bias,
        arrived + [own, oth, z_own, z_oth],
    )
    partial, low_own2, high_own2, low_oth, high_oth = lax.optimization_barrier(
        (partial, low_own2, high_own2, low_oth, high_oth)
    )
    c_own = corner(True, place, [low_own, low_own2], [high_own, high_own2])
    c_own, low_oth, high_oth = lax.optimization_barrier((c_own, low_oth, high_oth))
    c_oth = corner(False, place, [low_oth], [high_oth])
    c_own, c_oth = send(c_own, z_target(True)), send(c_oth, z_target(False))

    arrays = arrived + list(partial) + [low_own, low_own2, low_oth, high_own, high_own2, high_oth]
    half = jax.ShapeDtypeStruct((2, length, part), jnp.bfloat16)
    halo_keys = bias.shape[2] - OWN_KEYS
    middle, edge = [
        attend(
            functools.partial(halo_kernel, frames), half, (GROUP + 2, 2 * length, HDIM),
            2 * halo_keys, place, bias, arrays + corners,
        )
        for frames, corners in (((1, 2), []), ((0, 3), [c_own, c_oth]))
    ]
    by_frame = jnp.stack([edge[0], middle[0], middle[1], edge[1]])
    back = lax.all_to_all(by_frame, "frame", 0, 0, axis_index_groups=groups)
    result = pl.pallas_call(
        unpack_kernel,
        in_specs=[ANY],
        out_specs=ANY,
        out_shape=jax.ShapeDtypeStruct((length, width), jnp.bfloat16),
        scratch_shapes=[pltpu.SemaphoreType.DMA((GROUP,))],
        compiler_params=pltpu.CompilerParams(vmem_limit_bytes=4 * 2**20),
    )(back)
    return result[None]


def solution(mesh):
    sharded = P("frame", "row", None)
    body = functools.partial(shards, mesh.shape["frame"], mesh.shape["row"])
    return jax.shard_map(
        body, mesh=mesh, in_specs=(sharded, sharded, sharded, P()), out_specs=sharded, check_vma=False
    )
```

```python
import functools

import jax
import jax.numpy as jnp
import numpy as np
from jax import lax
from jax.experimental import pallas as pl
from jax.experimental.pallas import tpu as pltpu
from jax.sharding import PartitionSpec as P

HDIM = 128
BLK = 64
REACH = 2
NEG = -1e30
SCALE = HDIM ** -0.5 * 1.4426950408889634
AXES = ("frame", "row")
GROUP = 4
XN = 4
VMEM = pl.BlockSpec(memory_space=pltpu.VMEM)
SMEM = pl.BlockSpec(memory_space=pltpu.SMEM)
ANY = pl.BlockSpec(memory_space=pl.ANY)
FRAME_STEPS = (-2, -1, 0, 1, 2)
HALO_STEPS = (-1, 0, 1)
OWN_KEYS = 2 * BLK * len(FRAME_STEPS)


def pairs_of(frames, rows, target):
    pairs = []
    for frame in range(frames):
        for row in range(rows):
            to = target(frame, row)
            if to is not None and 0 <= to[0] < frames and 0 <= to[1] < rows:
                pairs.append((frame * rows + row, to[0] * rows + to[1]))
    return pairs


def key_block_table():
    own = [(step, block) for step in FRAME_STEPS for block in (0, 1)]
    halo = []
    for step in HALO_STEPS:
        reach = REACH - abs(step)
        halo += [(step, block) for block in range(-reach, 0)]
        halo += [(step, block) for block in range(2, 2 + reach)]
    return own + halo


def bias_of(radial_mask, frame_first, row_at, frame_total):
    table = key_block_table()
    offsets = 2 * REACH + 1
    pick = np.zeros((2, len(table), offsets * 2 * offsets), np.float32)
    for query in range(2):
        for at, (step, block) in enumerate(table):
            offset = block - query + REACH
            if 0 <= offset < offsets:
                pick[query, at, ((step + REACH) * 2 + query) * offsets + offset] = 1.0
    rows = lax.dynamic_slice_in_dim(radial_mask, row_at * 2, 2, 1)
    chosen = jnp.sum(jnp.asarray(pick) * rows.reshape(1, 1, -1).astype(jnp.float32), axis=2)
    steps = jnp.asarray(np.array([s for s, _ in table], np.int32))
    blocks = jnp.asarray(np.array([b for _, b in table], np.int32)) + row_at * 2
    inside = (blocks >= 0) & (blocks < radial_mask.shape[1])
    frames = frame_first + jnp.arange(GROUP, dtype=jnp.int32)[:, None] + steps[None, :]
    valid = (frames >= 0) & (frames < frame_total) & inside[None, :]
    allowed = (chosen[None] > 0) & valid[:, None, :]
    bias = jnp.where(allowed, 0.0, NEG).astype(jnp.float32)
    return jnp.repeat(bias, BLK, axis=2)


def pack_kernel(at_ref, q_ref, k_ref, v_ref, out0, out1, out2, out3, sems):
    me = at_ref[0]
    outs = (out0, out1, out2, out3)
    width = out0.shape[2]
    copies = []
    for slot in (1, 2, 3, 0):
        columns = pl.ds(pl.multiple_of((me ^ slot) * width, HDIM), width)
        for which, source in enumerate((k_ref, v_ref, q_ref)):
            copies.append(
                pltpu.make_async_copy(
                    source.at[:, columns], outs[slot].at[which], sems.at[slot, which]
                )
            )
    for copy in copies:
        copy.start()
    for copy in copies:
        copy.wait()


def unpack_kernel(in_ref, out_ref, sems):
    width = in_ref.shape[2]
    copies = [
        pltpu.make_async_copy(
            in_ref.at[part], out_ref.at[:, pl.ds(part * width, width)], sems.at[part]
        )
        for part in range(GROUP)
    ]
    for copy in copies:
        copy.start()
    for copy in copies:
        copy.wait()


def join_kernel(first, second, *rest):
    out, sems = rest[-2:]
    copies = [
        pltpu.make_async_copy(source.at[0:2], out.at[slot], sems.at[slot])
        for slot, source in enumerate((first, second))
    ]
    for copy in copies:
        copy.start()
    for copy in copies:
        copy.wait()


def join(first, second, *after):
    return pl.pallas_call(
        join_kernel,
        in_specs=[ANY] * (2 + len(after)),
        out_specs=VMEM,
        out_shape=jax.ShapeDtypeStruct((2, 2) + first.shape[1:], jnp.bfloat16),
        scratch_shapes=[pltpu.SemaphoreType.DMA((2,))],
        compiler_params=pltpu.CompilerParams(vmem_limit_bytes=4 * 2**20),
    )(first, second, *after)


def wrapped_kernel(at_ref, low, high, after, out, sem):
    del after
    x_at = at_ref[1]

    @pl.when(x_at == 0)
    def _():
        pltpu.make_async_copy(low, out, sem).start()

    @pl.when(x_at != 0)
    def _():
        pltpu.make_async_copy(high, out, sem).start()

    pltpu.make_async_copy(low, out, sem).wait()


def wrapped_of(place, low, high, after):
    return pl.pallas_call(
        wrapped_kernel,
        in_specs=[SMEM] + [ANY] * 3,
        out_specs=VMEM,
        out_shape=jax.ShapeDtypeStruct(low.shape, jnp.bfloat16),
        scratch_shapes=[pltpu.SemaphoreType.DMA(())],
        compiler_params=pltpu.CompilerParams(vmem_limit_bytes=4 * 2**20),
    )(place, low, high, after)


def corner_kernel(own_pair, at_ref, *refs):
    me, x_at = at_ref[0], at_ref[1]
    out, sems = refs[-2], refs[-1]
    lows, highs = refs[: (len(refs) - 2) // 2], refs[(len(refs) - 2) // 2 : -2]
    length = lows[0].shape[2]
    if own_pair:
        slot = jnp.where(me < 2, me, 3 - me)
    else:
        slot = jnp.where(me < 2, 1 - me, me - 2)

    def from_low(source):
        rows = pl.ds(length - BLK, BLK)
        return pltpu.make_async_copy(source.at[slot, :, rows], out.at[:, pl.ds(0, BLK)], sems.at[0])

    def from_high(source):
        rows = pl.ds(0, BLK)
        return pltpu.make_async_copy(source.at[slot, :, rows], out.at[:, pl.ds(BLK, BLK)], sems.at[1])

    @pl.when(x_at == 0)
    def _():
        from_low(lows[1]).start()

    @pl.when(x_at != 0)
    def _():
        from_low(lows[0]).start()

    @pl.when(x_at == XN - 1)
    def _():
        from_high(highs[1]).start()

    @pl.when(x_at != XN - 1)
    def _():
        from_high(highs[0]).start()

    from_low(lows[0]).wait()
    from_high(highs[0]).wait()


def corner(own_pair, place, lows, highs):
    shape = lows[0].shape
    return pl.pallas_call(
        functools.partial(corner_kernel, own_pair),
        in_specs=[SMEM] + [ANY] * (len(lows) + len(highs)),
        out_specs=VMEM,
        out_shape=jax.ShapeDtypeStruct((2, 2 * BLK, shape[3]), jnp.bfloat16),
        scratch_shapes=[pltpu.SemaphoreType.DMA((2,))],
        compiler_params=pltpu.CompilerParams(vmem_limit_bytes=4 * 2**20),
    )(place, *lows, *highs)


def head_scores(query, keys, bias):
    scores = jnp.concatenate(
        [
            lax.dot_general(query, k, (((1,), (1,)), ((), ())), preferred_element_type=jnp.float32)
            for k in keys
        ],
        axis=1,
    )
    return jnp.concatenate([scores[:BLK] + bias[0:1], scores[BLK:] + bias[1:2]], axis=0)


def own_bias(bias_ref, frame, near):
    start = (near[0] - frame + REACH) * 2 * BLK
    return bias_ref[frame, :, start : start + len(near) * 2 * BLK]


def weighted(weights, values):
    rounded = weights.astype(jnp.bfloat16)
    start, out = 0, 0
    for v in values:
        out = out + jnp.dot(
            rounded[:, start : start + v.shape[0]], v, preferred_element_type=jnp.float32
        )
        start += v.shape[0]
    return out


def gather_queries(me, queries, got):
    for slot, array in enumerate(got):
        queries[me ^ slot] = array[2]


def own_kernel(
    at_ref, bias_ref, got0, got1, got2, got3, own, oth, after0, after1, out_ref, top_ref, sum_ref, keys, values, queries,
):
    del after0, after1
    me = at_ref[0]
    gather_queries(me, queries, (got0, got1, got2, got3))
    for which, store in ((0, keys), (1, values)):
        for slot in range(2):
            store[me ^ slot] = own[slot, which]
            store[me ^ slot ^ 2] = oth[slot, which]
    near = [range(max(frame - REACH, 0), min(frame + REACH + 1, GROUP)) for frame in range(GROUP)]
    for head in range(own.shape[3] // HDIM):
        lanes = slice(head * HDIM, (head + 1) * HDIM)
        scores = [
            head_scores(
                queries[frame, :, lanes],
                [keys[at, :, lanes] for at in near[frame]],
                own_bias(bias_ref, frame, near[frame]),
            )
            for frame in range(GROUP)
        ]
        tops = [jnp.max(s, axis=1, keepdims=True) for s in scores]
        weights = [jnp.exp2((s - top) * SCALE) for s, top in zip(scores, tops)]
        totals = [jnp.sum(w, axis=1, keepdims=True) for w in weights]
        for frame in range(GROUP):
            out_ref[frame, :, lanes] = weighted(
                weights[frame], [values[at, :, lanes] for at in near[frame]]
            )
            shape = (tops[frame].shape[0], HDIM)
            top_ref[frame, :, lanes] = jnp.broadcast_to(tops[frame], shape)
            sum_ref[frame, :, lanes] = jnp.broadcast_to(totals[frame], shape)


def halo_kernel(
    frames, at_ref, bias_ref, got0, got1, got2, got3, sofar, top_in, sum_in,
    low_own, high_own, second, low_oth, high_oth, direct, z_own, z_oth, *rest
):
    corners, (out_ref, keys, values, queries, z_keys, z_values) = rest[:-6], rest[-6:]
    me, x_at = at_ref[0], at_ref[1]
    upper = me >= 2
    length = low_own.shape[2]
    below, above = slice(0, length), slice(length, 2 * length)
    gather_queries(me, queries, (got0, got1, got2, got3))
    for which, store in ((0, keys), (1, values)):
        for slot in range(2):
            at = 1 + (me ^ slot)
            store[at, below] = jnp.where(x_at == 0, second[slot, which], low_own[slot, which])
            store[at, above] = jnp.where(
                x_at == XN - 1, second[slot, which], high_own[slot, which]
            )
            at = 1 + (me ^ slot ^ 2)
            store[at, below] = jnp.where(x_at == 0, direct[slot, which], low_oth[slot, which])
            store[at, above] = jnp.where(x_at == XN - 1, direct[slot, which], high_oth[slot, which])
        z_store = z_keys if which == 0 else z_values
        for slot in range(2):
            at = me ^ slot
            z_store[jnp.where(upper, at - 2, at + 2)] = z_own[slot, which]
            at = at ^ 2
            z_store[jnp.where(upper, at + 2, at - 2)] = z_oth[slot, which]
        for arrived, at in zip(corners, (jnp.where(upper, 0, 5), jnp.where(upper, 5, 0))):
            store[at, length - BLK : length + BLK] = arrived[which]
    reaches = [(step, (REACH - abs(step)) * BLK) for step in HALO_STEPS]
    units = [
        (at, frame, slice(head * HDIM, (head + 1) * HDIM))
        for head in range(low_own.shape[3] // HDIM)
        for at, frame in enumerate(frames)
    ]

    z_frames = (-2, -1, GROUP, GROUP + 1)
    z_near = [[z for z in z_frames if abs(z - frame) <= REACH] for frame in range(GROUP)]

    def spans(store, z_store, frame, lanes):
        return [z_store[z_frames.index(z), :, lanes] for z in z_near[frame]] + [
            store[frame + 1 + step, length - reach : length + reach, lanes]
            for step, reach in reaches
        ]

    biases = {
        frame: jnp.concatenate(
            [own_bias(bias_ref, frame, z_near[frame]), bias_ref[frame, :, OWN_KEYS:]], axis=1
        )
        for frame in frames
    }
    scores = [
        head_scores(queries[frame, :, lanes], spans(keys, z_keys, frame, lanes), biases[frame])
        for _, frame, lanes in units
    ]
    tops = [
        jnp.maximum(top_in[frame, :, lanes], jnp.max(s, axis=1, keepdims=True))
        for s, (_, frame, lanes) in zip(scores, units)
    ]
    weights = [jnp.exp2((s - top[:, 0:1]) * SCALE) for s, top in zip(scores, tops)]
    totals = [jnp.sum(w, axis=1, keepdims=True) for w in weights]
    for top, w, total, (at, frame, lanes) in zip(tops, weights, totals, units):
        again = jnp.exp2((top_in[frame, :, lanes] - top) * SCALE)
        out = sofar[frame, :, lanes] * again + weighted(
            w, spans(values, z_values, frame, lanes)
        )
        total = sum_in[frame, :, lanes] * again + total
        out_ref[at, :, lanes] = (out / total).astype(jnp.bfloat16)


def attend(kernel, out_shape, scratches, work, place, bias, arrays, after=()):
    length, width = arrays[0].shape[1:]
    return pl.pallas_call(
        kernel,
        in_specs=[SMEM] + [VMEM] * (1 + len(arrays)) + [ANY] * len(after),
        out_specs=jax.tree.map(lambda _: VMEM, out_shape),
        out_shape=out_shape,
        scratch_shapes=[pltpu.VMEM(scratch, jnp.bfloat16) for scratch in scratches],
        compiler_params=pltpu.CompilerParams(vmem_limit_bytes=24 * 2**20),
        cost_estimate=pl.CostEstimate(
            flops=4 * work * width * length, bytes_accessed=8_000_000,
            transcendentals=work * width * length // HDIM,
        ),
    )(place, bias, *arrays, *after)


def shards(frame_total, row_total, queries, key_states, value_states, radial_mask):
    length, width = queries.shape[1:]
    part = width // GROUP
    frame_at = lax.axis_index("frame")
    row_at = lax.axis_index("row")
    me = frame_at % GROUP
    x_at = row_at % XN
    place = jnp.stack([me, x_at]).astype(jnp.int32)

    def send(array, target):
        return lax.ppermute(array, AXES, pairs_of(frame_total, row_total, target))

    packed = pl.pallas_call(
        pack_kernel,
        in_specs=[SMEM] + [ANY] * 3,
        out_specs=[VMEM] * GROUP,
        out_shape=[jax.ShapeDtypeStruct((3, length, part), jnp.bfloat16)] * GROUP,
        scratch_shapes=[pltpu.SemaphoreType.DMA((GROUP, 3))],
        compiler_params=pltpu.CompilerParams(vmem_limit_bytes=56 * 2**20),
    )(place, queries[0], key_states[0], value_states[0])

    def flip(bits):
        return lambda f, r: (f ^ bits, r)

    groups = [list(range(f, f + GROUP)) for f in range(0, frame_total, GROUP)]
    arrived = [packed[0]] + [send(packed[s], flip(s)) for s in range(1, GROUP)]
    own = jnp.stack([arrived[0][:2], arrived[1][:2]])

    def row_first(by):
        edge = XN - 1 if by > 0 else 0
        return lambda f, r: (f, r + by) if r % XN != edge else (f, r - by * (XN - 1))

    def row_second(f, r):
        return (f, r + XN) if r % XN == 0 else (f, r - XN) if r % XN == XN - 1 else None

    def row_inner(by):
        edge = XN - 1 if by > 0 else 0
        return lambda f, r: (f, r + by) if r % XN != edge else None

    def row_across(f, r):
        return (f, r + 1) if r % XN == XN - 1 else (f, r - 1) if r % XN == 0 else None

    def z_target(own_pair):
        def target(f, r):
            up = (f % GROUP >= 2) == own_pair
            return (f + GROUP if up else f - GROUP, r)

        return target

    low_own, high_own = send(own, row_first(1)), send(own, row_first(-1))
    z_own = send(own, z_target(True))
    oth = join(arrived[2], arrived[3])
    direct = send(oth, row_across)
    wrapped = wrapped_of(place, low_own, high_own, oth)
    second = send(wrapped, row_second)

    bias = bias_of(radial_mask, frame_at - me, row_at, frame_total)
    sums = [jax.ShapeDtypeStruct((GROUP, length, part), jnp.float32)] * 3
    partial = attend(
        own_kernel, sums, [(GROUP, length, part)] * 3, 14 * length, place, bias,
        arrived + [own, oth], [wrapped, z_own],
    )
    later = join(arrived[2], arrived[3], partial[0])
    low_oth, high_oth = send(later, row_inner(1)), send(later, row_inner(-1))
    z_oth = send(later, z_target(False))
    c_own = corner(True, place, [low_own, second], [high_own, second])
    c_oth = corner(False, place, [low_oth, direct], [high_oth, direct])
    c_own, c_oth = send(c_own, z_target(True)), send(c_oth, z_target(False))

    arrays = arrived + list(partial) + [low_own, high_own, second, low_oth, high_oth, direct]
    arrays += [z_own, z_oth]
    group_shape = (GROUP, length, part)
    half = jax.ShapeDtypeStruct((2, length, part), jnp.bfloat16)
    halo_keys = bias.shape[2] - OWN_KEYS
    middle, edge = [
        attend(
            functools.partial(halo_kernel, frames), half,
            [(GROUP + 2, 2 * length, part)] * 2 + [group_shape] * 3, 2 * halo_keys, place, bias, arrays + corners,
        )
        for frames, corners in (((1, 2), []), ((0, 3), [c_own, c_oth]))
    ]
    by_frame = jnp.stack([edge[0], middle[0], middle[1], edge[1]])
    back = lax.all_to_all(by_frame, "frame", 0, 0, axis_index_groups=groups)
    result = pl.pallas_call(
        unpack_kernel,
        in_specs=[ANY],
        out_specs=ANY,
        out_shape=jax.ShapeDtypeStruct((length, width), jnp.bfloat16),
        scratch_shapes=[pltpu.SemaphoreType.DMA((GROUP,))],
        compiler_params=pltpu.CompilerParams(vmem_limit_bytes=4 * 2**20),
    )(back)
    return result[None]


def solution(mesh):
    sharded = P("frame", "row", None)
    body = functools.partial(shards, mesh.shape["frame"], mesh.shape["row"])
    return jax.shard_map(
        body, mesh=mesh, in_specs=(sharded, sharded, sharded, P()), out_specs=sharded, check_vma=False
    )
```

```python
import functools

import jax
import jax.numpy as jnp
import numpy as np
from jax import lax
from jax.experimental import pallas as pl
from jax.experimental.pallas import tpu as pltpu
from jax.sharding import PartitionSpec as P

HDIM = 128
BLK = 64
REACH = 2
NEG = -1e30
SCALE = HDIM ** -0.5 * 1.4426950408889634
AXES = ("frame", "row")
GROUP = 4
XN = 4
VMEM = pl.BlockSpec(memory_space=pltpu.VMEM)
SMEM = pl.BlockSpec(memory_space=pltpu.SMEM)
ANY = pl.BlockSpec(memory_space=pl.ANY)
FRAME_STEPS = (-2, -1, 0, 1, 2)
HALO_STEPS = (-1, 0, 1)
OWN_KEYS = 2 * BLK * len(FRAME_STEPS)


def pairs_of(frames, rows, target):
    pairs = []
    for frame in range(frames):
        for row in range(rows):
            to = target(frame, row)
            if to is not None and 0 <= to[0] < frames and 0 <= to[1] < rows:
                pairs.append((frame * rows + row, to[0] * rows + to[1]))
    return pairs


def key_block_table():
    own = [(step, block) for step in FRAME_STEPS for block in (0, 1)]
    halo = []
    for step in HALO_STEPS:
        reach = REACH - abs(step)
        halo += [(step, block) for block in range(-reach, 0)]
        halo += [(step, block) for block in range(2, 2 + reach)]
    return own + halo


def bias_of(radial_mask, frame_first, row_at, frame_total):
    table = key_block_table()
    offsets = 2 * REACH + 1
    pick = np.zeros((2, len(table), offsets * 2 * offsets), np.float32)
    for query in range(2):
        for at, (step, block) in enumerate(table):
            offset = block - query + REACH
            if 0 <= offset < offsets:
                pick[query, at, ((step + REACH) * 2 + query) * offsets + offset] = 1.0
    rows = lax.dynamic_slice_in_dim(radial_mask, row_at * 2, 2, 1)
    chosen = jnp.sum(jnp.asarray(pick) * rows.reshape(1, 1, -1).astype(jnp.float32), axis=2)
    steps = jnp.asarray(np.array([s for s, _ in table], np.int32))
    blocks = jnp.asarray(np.array([b for _, b in table], np.int32)) + row_at * 2
    inside = (blocks >= 0) & (blocks < radial_mask.shape[1])
    frames = frame_first + jnp.arange(GROUP, dtype=jnp.int32)[:, None] + steps[None, :]
    valid = (frames >= 0) & (frames < frame_total) & inside[None, :]
    allowed = (chosen[None] > 0) & valid[:, None, :]
    bias = jnp.where(allowed, 0.0, NEG).astype(jnp.float32)
    return jnp.repeat(bias, BLK, axis=2)


def pack_kernel(q_ref, k_ref, v_ref, out0, out1, out2, out3, sems):
    me = lax.axis_index("frame") % GROUP
    outs = (out0, out1, out2, out3)
    width = out0.shape[2]
    copies = []
    for slot in (1, 2, 3, 0):
        columns = pl.ds(pl.multiple_of((me ^ slot) * width, HDIM), width)
        for which, source in enumerate((k_ref, v_ref, q_ref)):
            copies.append(
                pltpu.make_async_copy(
                    source.at[:, columns], outs[slot].at[which], sems.at[slot, which]
                )
            )
    for copy in copies:
        copy.start()
    for copy in copies:
        copy.wait()


def unpack_kernel(in_ref, out_ref, sems):
    width = in_ref.shape[2]
    copies = [
        pltpu.make_async_copy(
            in_ref.at[part], out_ref.at[:, pl.ds(part * width, width)], sems.at[part]
        )
        for part in range(GROUP)
    ]
    for copy in copies:
        copy.start()
    for copy in copies:
        copy.wait()


def join_kernel(first, second, *rest):
    out, sems = rest[-2:]
    copies = [
        pltpu.make_async_copy(source.at[0:2], out.at[slot], sems.at[slot])
        for slot, source in enumerate((first, second))
    ]
    for copy in copies:
        copy.start()
    for copy in copies:
        copy.wait()


def join(first, second, *after):
    return pl.pallas_call(
        join_kernel,
        in_specs=[ANY] * (2 + len(after)),
        out_specs=VMEM,
        out_shape=jax.ShapeDtypeStruct((2, 2) + first.shape[1:], jnp.bfloat16),
        scratch_shapes=[pltpu.SemaphoreType.DMA((2,))],
        compiler_params=pltpu.CompilerParams(vmem_limit_bytes=4 * 2**20),
    )(first, second, *after)


def wrapped_kernel(at_ref, low, high, after, out, sem):
    del after
    x_at = at_ref[1]

    @pl.when(x_at == 0)
    def _():
        pltpu.make_async_copy(low, out, sem).start()

    @pl.when(x_at != 0)
    def _():
        pltpu.make_async_copy(high, out, sem).start()

    pltpu.make_async_copy(low, out, sem).wait()


def wrapped_of(place, low, high, after):
    return pl.pallas_call(
        wrapped_kernel,
        in_specs=[SMEM] + [ANY] * 3,
        out_specs=VMEM,
        out_shape=jax.ShapeDtypeStruct(low.shape, jnp.bfloat16),
        scratch_shapes=[pltpu.SemaphoreType.DMA(())],
        compiler_params=pltpu.CompilerParams(vmem_limit_bytes=4 * 2**20),
    )(place, low, high, after)


def corner_kernel(
    at_ref, low_own, high_own, second, low_oth, high_oth, direct, out_own, out_oth, sems
):
    me, x_at = at_ref[0], at_ref[1]
    length = low_own.shape[2]
    own = (jnp.where(me < 2, me, 3 - me), out_own, 0)
    oth = (jnp.where(me < 2, 1 - me, me - 2), out_oth, 2)

    def from_low(source, slot, out, sem):
        rows = pl.ds(length - BLK, BLK)
        return pltpu.make_async_copy(source.at[slot, :, rows], out.at[:, pl.ds(0, BLK)], sems.at[sem])

    def from_high(source, slot, out, sem):
        rows = pl.ds(0, BLK)
        return pltpu.make_async_copy(
            source.at[slot, :, rows], out.at[:, pl.ds(BLK, BLK)], sems.at[sem + 1]
        )

    @pl.when(x_at == 0)
    def _():
        from_low(second, *own).start()
        from_low(direct, *oth).start()

    @pl.when(x_at != 0)
    def _():
        from_low(low_own, *own).start()
        from_low(low_oth, *oth).start()

    @pl.when(x_at == XN - 1)
    def _():
        from_high(second, *own).start()
        from_high(direct, *oth).start()

    @pl.when(x_at != XN - 1)
    def _():
        from_high(high_own, *own).start()
        from_high(high_oth, *oth).start()

    from_low(low_own, *own).wait()
    from_high(high_own, *own).wait()
    from_low(low_oth, *oth).wait()
    from_high(high_oth, *oth).wait()


def corners_of(place, *arrays):
    shape = jax.ShapeDtypeStruct((2, 2 * BLK, arrays[0].shape[3]), jnp.bfloat16)
    return pl.pallas_call(
        corner_kernel,
        in_specs=[SMEM] + [ANY] * len(arrays),
        out_specs=[VMEM] * 2,
        out_shape=[shape] * 2,
        scratch_shapes=[pltpu.SemaphoreType.DMA((4,))],
        compiler_params=pltpu.CompilerParams(vmem_limit_bytes=4 * 2**20),
    )(place, *arrays)


def head_scores(query, keys, bias):
    scores = jnp.concatenate(
        [
            lax.dot_general(query, k, (((1,), (1,)), ((), ())), preferred_element_type=jnp.float32)
            for k in keys
        ],
        axis=1,
    )
    return jnp.concatenate([scores[:BLK] + bias[0:1], scores[BLK:] + bias[1:2]], axis=0)


def own_bias(bias_ref, frame, near):
    start = (near[0] - frame + REACH) * 2 * BLK
    return bias_ref[frame, :, start : start + len(near) * 2 * BLK]


def weighted(weights, values):
    rounded = weights.astype(jnp.bfloat16)
    start, out = 0, 0
    for v in values:
        out = out + jnp.dot(
            rounded[:, start : start + v.shape[0]], v, preferred_element_type=jnp.float32
        )
        start += v.shape[0]
    return out


def gather_queries(me, queries, got):
    for slot, array in enumerate(got):
        queries[me ^ slot] = array[2]


def own_kernel(
    at_ref, bias_ref, got0, got1, got2, got3, own, oth, after0, after1, out_ref, top_ref, sum_ref, keys, values, queries,
):
    del after0, after1
    me = at_ref[0]
    gather_queries(me, queries, (got0, got1, got2, got3))
    for which, store in ((0, keys), (1, values)):
        for slot in range(2):
            store[me ^ slot] = own[slot, which]
            store[me ^ slot ^ 2] = oth[slot, which]
    near = [range(max(frame - REACH, 0), min(frame + REACH + 1, GROUP)) for frame in range(GROUP)]
    for head in range(own.shape[3] // HDIM):
        lanes = slice(head * HDIM, (head + 1) * HDIM)
        scores = [
            head_scores(
                queries[frame, :, lanes],
                [keys[at, :, lanes] for at in near[frame]],
                own_bias(bias_ref, frame, near[frame]),
            )
            for frame in range(GROUP)
        ]
        tops = [jnp.max(s, axis=1, keepdims=True) for s in scores]
        weights = [jnp.exp2((s - top) * SCALE) for s, top in zip(scores, tops)]
        totals = [jnp.sum(w, axis=1, keepdims=True) for w in weights]
        for frame in range(GROUP):
            out_ref[frame, :, lanes] = weighted(
                weights[frame], [values[at, :, lanes] for at in near[frame]]
            )
            shape = (tops[frame].shape[0], HDIM)
            top_ref[frame, :, lanes] = jnp.broadcast_to(tops[frame], shape)
            sum_ref[frame, :, lanes] = jnp.broadcast_to(totals[frame], shape)


def halo_kernel(
    frames, at_ref, bias_ref, got0, got1, got2, got3, sofar, top_in, sum_in,
    low_own, high_own, second, low_oth, high_oth, direct, z_own, z_oth, *rest
):
    corners, (out_ref, keys, values, queries, z_keys, z_values) = rest[:-6], rest[-6:]
    me, x_at = at_ref[0], at_ref[1]
    upper = me >= 2
    length = low_own.shape[2]
    below, above = slice(0, length), slice(length, 2 * length)
    gather_queries(me, queries, (got0, got1, got2, got3))
    for which, store in ((0, keys), (1, values)):
        for slot in range(2):
            at = 1 + (me ^ slot)
            store[at, below] = jnp.where(x_at == 0, second[slot, which], low_own[slot, which])
            store[at, above] = jnp.where(
                x_at == XN - 1, second[slot, which], high_own[slot, which]
            )
            at = 1 + (me ^ slot ^ 2)
            store[at, below] = jnp.where(x_at == 0, direct[slot, which], low_oth[slot, which])
            store[at, above] = jnp.where(x_at == XN - 1, direct[slot, which], high_oth[slot, which])
        z_store = z_keys if which == 0 else z_values
        for slot in range(2):
            at = me ^ slot
            z_store[jnp.where(upper, at - 2, at + 2)] = z_own[slot, which]
            at = at ^ 2
            z_store[jnp.where(upper, at + 2, at - 2)] = z_oth[slot, which]
        for arrived, at in zip(corners, (jnp.where(upper, 0, 5), jnp.where(upper, 5, 0))):
            store[at, length - BLK : length + BLK] = arrived[which]
    reaches = [(step, (REACH - abs(step)) * BLK) for step in HALO_STEPS]
    units = [
        (at, frame, slice(head * HDIM, (head + 1) * HDIM))
        for head in range(low_own.shape[3] // HDIM)
        for at, frame in enumerate(frames)
    ]

    z_frames = (-2, -1, GROUP, GROUP + 1)
    z_near = [[z for z in z_frames if abs(z - frame) <= REACH] for frame in range(GROUP)]

    def spans(store, z_store, frame, lanes):
        return [z_store[z_frames.index(z), :, lanes] for z in z_near[frame]] + [
            store[frame + 1 + step, length - reach : length + reach, lanes]
            for step, reach in reaches
        ]

    biases = {
        frame: jnp.concatenate(
            [own_bias(bias_ref, frame, z_near[frame]), bias_ref[frame, :, OWN_KEYS:]], axis=1
        )
        for frame in frames
    }
    scores = [
        head_scores(queries[frame, :, lanes], spans(keys, z_keys, frame, lanes), biases[frame])
        for _, frame, lanes in units
    ]
    tops = [
        jnp.maximum(top_in[frame, :, lanes], jnp.max(s, axis=1, keepdims=True))
        for s, (_, frame, lanes) in zip(scores, units)
    ]
    weights = [jnp.exp2((s - top[:, 0:1]) * SCALE) for s, top in zip(scores, tops)]
    totals = [jnp.sum(w, axis=1, keepdims=True) for w in weights]
    for top, w, total, (at, frame, lanes) in zip(tops, weights, totals, units):
        again = jnp.exp2((top_in[frame, :, lanes] - top) * SCALE)
        out = sofar[frame, :, lanes] * again + weighted(
            w, spans(values, z_values, frame, lanes)
        )
        total = sum_in[frame, :, lanes] * again + total
        out_ref[at, :, lanes] = (out / total).astype(jnp.bfloat16)


def attend(kernel, out_shape, scratches, work, place, bias, arrays, after=()):
    length, width = arrays[0].shape[1:]
    return pl.pallas_call(
        kernel,
        in_specs=[SMEM] + [VMEM] * (1 + len(arrays)) + [ANY] * len(after),
        out_specs=jax.tree.map(lambda _: VMEM, out_shape),
        out_shape=out_shape,
        scratch_shapes=[pltpu.VMEM(scratch, jnp.bfloat16) for scratch in scratches],
        compiler_params=pltpu.CompilerParams(vmem_limit_bytes=24 * 2**20),
        cost_estimate=pl.CostEstimate(
            flops=4 * work * width * length, bytes_accessed=8_000_000,
            transcendentals=work * width * length // HDIM,
        ),
    )(place, bias, *arrays, *after)


def shards(frame_total, row_total, queries, key_states, value_states, radial_mask):
    length, width = queries.shape[1:]
    part = width // GROUP
    frame_at = lax.axis_index("frame")
    row_at = lax.axis_index("row")
    me = frame_at % GROUP
    x_at = row_at % XN
    place = jnp.stack([me, x_at]).astype(jnp.int32)

    def send(array, target):
        return lax.ppermute(array, AXES, pairs_of(frame_total, row_total, target))

    packed = pl.pallas_call(
        pack_kernel,
        in_specs=[ANY] * 3,
        out_specs=[VMEM] * GROUP,
        out_shape=[jax.ShapeDtypeStruct((3, length, part), jnp.bfloat16)] * GROUP,
        scratch_shapes=[pltpu.SemaphoreType.DMA((GROUP, 3))],
        compiler_params=pltpu.CompilerParams(vmem_limit_bytes=56 * 2**20),
    )(queries[0], key_states[0], value_states[0])

    def flip(bits):
        return lambda f, r: (f ^ bits, r)

    groups = [list(range(f, f + GROUP)) for f in range(0, frame_total, GROUP)]
    arrived = [packed[0]] + [send(packed[s], flip(s)) for s in range(1, GROUP)]
    own = jnp.stack([arrived[0][:2], arrived[1][:2]])

    def row_first(by):
        edge = XN - 1 if by > 0 else 0
        return lambda f, r: (f, r + by) if r % XN != edge else (f, r - by * (XN - 1))

    def row_second(f, r):
        return (f, r + XN) if r % XN == 0 else (f, r - XN) if r % XN == XN - 1 else None

    def row_inner(by):
        edge = XN - 1 if by > 0 else 0
        return lambda f, r: (f, r + by) if r % XN != edge else None

    def row_across(f, r):
        return (f, r + 1) if r % XN == XN - 1 else (f, r - 1) if r % XN == 0 else None

    def z_target(own_pair):
        def target(f, r):
            up = (f % GROUP >= 2) == own_pair
            return (f + GROUP if up else f - GROUP, r)

        return target

    low_own, high_own = send(own, row_first(1)), send(own, row_first(-1))
    z_own = send(own, z_target(True))
    oth = join(arrived[2], arrived[3])
    direct = send(oth, row_across)
    wrapped = wrapped_of(place, low_own, high_own, oth)
    second = send(wrapped, row_second)

    bias = bias_of(radial_mask, frame_at - me, row_at, frame_total)
    sums = [jax.ShapeDtypeStruct((GROUP, length, part), jnp.float32)] * 3
    partial = attend(
        own_kernel, sums, [(GROUP, length, part)] * 3, 14 * length, place, bias,
        arrived + [own, oth], [wrapped, z_own],
    )
    later = join(arrived[2], arrived[3], partial[0])
    low_oth, high_oth = send(later, row_inner(1)), send(later, row_inner(-1))
    z_oth = send(later, z_target(False))
    c_own, c_oth = corners_of(place, low_own, high_own, second, low_oth, high_oth, direct)
    c_own, c_oth = send(c_own, z_target(True)), send(c_oth, z_target(False))

    arrays = arrived + list(partial) + [low_own, high_own, second, low_oth, high_oth, direct]
    arrays += [z_own, z_oth]
    group_shape = (GROUP, length, part)
    half = jax.ShapeDtypeStruct((2, length, part), jnp.bfloat16)
    halo_keys = bias.shape[2] - OWN_KEYS
    middle, edge = [
        attend(
            functools.partial(halo_kernel, frames), half,
            [(GROUP + 2, 2 * length, part)] * 2 + [group_shape] * 3, 2 * halo_keys, place, bias, arrays + corners,
        )
        for frames, corners in (((1, 2), []), ((0, 3), [c_own, c_oth]))
    ]
    by_frame = jnp.stack([edge[0], middle[0], middle[1], edge[1]])
    back = lax.all_to_all(by_frame, "frame", 0, 0, axis_index_groups=groups)
    result = pl.pallas_call(
        unpack_kernel,
        in_specs=[ANY],
        out_specs=ANY,
        out_shape=jax.ShapeDtypeStruct((length, width), jnp.bfloat16),
        scratch_shapes=[pltpu.SemaphoreType.DMA((GROUP,))],
        compiler_params=pltpu.CompilerParams(vmem_limit_bytes=4 * 2**20),
    )(back)
    return result[None]


def solution(mesh):
    sharded = P("frame", "row", None)
    body = functools.partial(shards, mesh.shape["frame"], mesh.shape["row"])
    return jax.shard_map(
        body, mesh=mesh, in_specs=(sharded, sharded, sharded, P()), out_specs=sharded, check_vma=False
    )
```

```python
import functools

import jax
import jax.numpy as jnp
import numpy as np
from jax import lax
from jax.experimental import pallas as pl
from jax.experimental.pallas import tpu as pltpu
from jax.sharding import PartitionSpec as P

HDIM = 128
BLK = 64
REACH = 2
NEG = -1e30
SCALE = HDIM ** -0.5 * 1.4426950408889634
AXES = ("frame", "row")
GROUP = 4
XN = 4
VMEM = pl.BlockSpec(memory_space=pltpu.VMEM)
SMEM = pl.BlockSpec(memory_space=pltpu.SMEM)
ANY = pl.BlockSpec(memory_space=pl.ANY)
FRAME_STEPS = (-2, -1, 0, 1, 2)
HALO_STEPS = (-1, 0, 1)
OWN_KEYS = 2 * BLK * len(FRAME_STEPS)


def pairs_of(frames, rows, target):
    pairs = []
    for frame in range(frames):
        for row in range(rows):
            to = target(frame, row)
            if to is not None and 0 <= to[0] < frames and 0 <= to[1] < rows:
                pairs.append((frame * rows + row, to[0] * rows + to[1]))
    return pairs


def key_block_table():
    own = [(step, block) for step in FRAME_STEPS for block in (0, 1)]
    halo = []
    for step in HALO_STEPS:
        reach = REACH - abs(step)
        halo += [(step, block) for block in range(-reach, 0)]
        halo += [(step, block) for block in range(2, 2 + reach)]
    return own + halo


def bias_of(radial_mask, frame_first, row_at, frame_total):
    table = key_block_table()
    offsets = 2 * REACH + 1
    pick = np.zeros((2, len(table), offsets * 2 * offsets), np.float32)
    for query in range(2):
        for at, (step, block) in enumerate(table):
            offset = block - query + REACH
            if 0 <= offset < offsets:
                pick[query, at, ((step + REACH) * 2 + query) * offsets + offset] = 1.0
    rows = lax.dynamic_slice_in_dim(radial_mask, row_at * 2, 2, 1)
    chosen = jnp.sum(jnp.asarray(pick) * rows.reshape(1, 1, -1).astype(jnp.float32), axis=2)
    steps = jnp.asarray(np.array([s for s, _ in table], np.int32))
    blocks = jnp.asarray(np.array([b for _, b in table], np.int32)) + row_at * 2
    inside = (blocks >= 0) & (blocks < radial_mask.shape[1])
    frames = frame_first + jnp.arange(GROUP, dtype=jnp.int32)[:, None] + steps[None, :]
    valid = (frames >= 0) & (frames < frame_total) & inside[None, :]
    allowed = (chosen[None] > 0) & valid[:, None, :]
    bias = jnp.where(allowed, 0.0, NEG).astype(jnp.float32)
    return jnp.repeat(bias, BLK, axis=2)


def pack_kernel(q_ref, k_ref, v_ref, out0, out1, out2, out3, sems):
    me = lax.axis_index("frame") % GROUP
    outs = (out0, out1, out2, out3)
    width = out0.shape[2]
    copies = []
    for slot in (1, 2, 3, 0):
        columns = pl.ds(pl.multiple_of((me ^ slot) * width, HDIM), width)
        for which, source in enumerate((k_ref, v_ref, q_ref)):
            copies.append(
                pltpu.make_async_copy(
                    source.at[:, columns], outs[slot].at[which], sems.at[slot, which]
                )
            )
    for copy in copies:
        copy.start()
    for copy in copies:
        copy.wait()


def unpack_kernel(in_ref, out_ref, sems):
    width = in_ref.shape[2]
    copies = [
        pltpu.make_async_copy(
            in_ref.at[part], out_ref.at[:, pl.ds(part * width, width)], sems.at[part]
        )
        for part in range(GROUP)
    ]
    for copy in copies:
        copy.start()
    for copy in copies:
        copy.wait()


def join_kernel(first, second, *rest):
    out, sems = rest[-2:]
    copies = [
        pltpu.make_async_copy(source.at[0:2], out.at[slot], sems.at[slot])
        for slot, source in enumerate((first, second))
    ]
    for copy in copies:
        copy.start()
    for copy in copies:
        copy.wait()


def join(first, second, *after):
    return pl.pallas_call(
        join_kernel,
        in_specs=[ANY] * (2 + len(after)),
        out_specs=VMEM,
        out_shape=jax.ShapeDtypeStruct((2, 2) + first.shape[1:], jnp.bfloat16),
        scratch_shapes=[pltpu.SemaphoreType.DMA((2,))],
        compiler_params=pltpu.CompilerParams(vmem_limit_bytes=4 * 2**20),
    )(first, second, *after)


def wrapped_kernel(at_ref, low, high, after, out, sem):
    del after
    x_at = at_ref[1]

    @pl.when(x_at == 0)
    def _():
        pltpu.make_async_copy(low, out, sem).start()

    @pl.when(x_at != 0)
    def _():
        pltpu.make_async_copy(high, out, sem).start()

    pltpu.make_async_copy(low, out, sem).wait()


def wrapped_of(place, low, high, after):
    return pl.pallas_call(
        wrapped_kernel,
        in_specs=[SMEM] + [ANY] * 3,
        out_specs=VMEM,
        out_shape=jax.ShapeDtypeStruct(low.shape, jnp.bfloat16),
        scratch_shapes=[pltpu.SemaphoreType.DMA(())],
        compiler_params=pltpu.CompilerParams(vmem_limit_bytes=4 * 2**20),
    )(place, low, high, after)


def corner_kernel(
    at_ref, low_own, high_own, second, low_oth, high_oth, direct, out_own, out_oth, sems
):
    me, x_at = at_ref[0], at_ref[1]
    length = low_own.shape[2]
    own = (jnp.where(me < 2, me, 3 - me), out_own, 0)
    oth = (jnp.where(me < 2, 1 - me, me - 2), out_oth, 2)

    def from_low(source, slot, out, sem):
        rows = pl.ds(length - BLK, BLK)
        return pltpu.make_async_copy(source.at[slot, :, rows], out.at[:, pl.ds(0, BLK)], sems.at[sem])

    def from_high(source, slot, out, sem):
        rows = pl.ds(0, BLK)
        return pltpu.make_async_copy(
            source.at[slot, :, rows], out.at[:, pl.ds(BLK, BLK)], sems.at[sem + 1]
        )

    @pl.when(x_at == 0)
    def _():
        from_low(second, *own).start()
        from_low(direct, *oth).start()

    @pl.when(x_at != 0)
    def _():
        from_low(low_own, *own).start()
        from_low(low_oth, *oth).start()

    @pl.when(x_at == XN - 1)
    def _():
        from_high(second, *own).start()
        from_high(direct, *oth).start()

    @pl.when(x_at != XN - 1)
    def _():
        from_high(high_own, *own).start()
        from_high(high_oth, *oth).start()

    from_low(low_own, *own).wait()
    from_high(high_own, *own).wait()
    from_low(low_oth, *oth).wait()
    from_high(high_oth, *oth).wait()


def corners_of(place, *arrays):
    shape = jax.ShapeDtypeStruct((2, 2 * BLK, arrays[0].shape[3]), jnp.bfloat16)
    return pl.pallas_call(
        corner_kernel,
        in_specs=[SMEM] + [ANY] * len(arrays),
        out_specs=[VMEM] * 2,
        out_shape=[shape] * 2,
        scratch_shapes=[pltpu.SemaphoreType.DMA((4,))],
        compiler_params=pltpu.CompilerParams(vmem_limit_bytes=4 * 2**20),
    )(place, *arrays)


def head_scores(query, keys, bias):
    scores = jnp.concatenate(
        [
            lax.dot_general(query, k, (((1,), (1,)), ((), ())), preferred_element_type=jnp.float32)
            for k in keys
        ],
        axis=1,
    )
    return jnp.concatenate([scores[:BLK] + bias[0:1], scores[BLK:] + bias[1:2]], axis=0)


def own_bias(bias_ref, frame, near):
    start = (near[0] - frame + REACH) * 2 * BLK
    return bias_ref[frame, :, start : start + len(near) * 2 * BLK]


def weighted(weights, values):
    rounded = weights.astype(jnp.bfloat16)
    start, out = 0, 0
    for v in values:
        out = out + jnp.dot(
            rounded[:, start : start + v.shape[0]], v, preferred_element_type=jnp.float32
        )
        start += v.shape[0]
    return out


def gather_queries(me, queries, got):
    for slot, array in enumerate(got):
        queries[me ^ slot] = array[2]


def own_kernel(
    at_ref, bias_ref, got0, got1, got2, got3, own, oth, after0, after1, out_ref, top_ref, sum_ref, keys, values, queries,
):
    del after0, after1
    me = at_ref[0]
    gather_queries(me, queries, (got0, got1, got2, got3))
    for which, store in ((0, keys), (1, values)):
        for slot in range(2):
            store[me ^ slot] = own[slot, which]
            store[me ^ slot ^ 2] = oth[slot, which]
    near = [range(max(frame - REACH, 0), min(frame + REACH + 1, GROUP)) for frame in range(GROUP)]
    for head in range(own.shape[3] // HDIM):
        lanes = slice(head * HDIM, (head + 1) * HDIM)
        scores = [
            head_scores(
                queries[frame, :, lanes],
                [keys[at, :, lanes] for at in near[frame]],
                own_bias(bias_ref, frame, near[frame]),
            )
            for frame in range(GROUP)
        ]
        tops = [jnp.max(s, axis=1, keepdims=True) for s in scores]
        weights = [jnp.exp2((s - top) * SCALE) for s, top in zip(scores, tops)]
        totals = [jnp.sum(w, axis=1, keepdims=True) for w in weights]
        for frame in range(GROUP):
            out_ref[frame, :, lanes] = weighted(
                weights[frame], [values[at, :, lanes] for at in near[frame]]
            )
            shape = (tops[frame].shape[0], HDIM)
            top_ref[frame, :, lanes] = jnp.broadcast_to(tops[frame], shape)
            sum_ref[frame, :, lanes] = jnp.broadcast_to(totals[frame], shape)


def halo_kernel(
    frames, at_ref, bias_ref, got0, got1, got2, got3, sofar, top_in, sum_in,
    low_own, high_own, second, low_oth, high_oth, direct, z_own, z_oth, *rest
):
    corners, (out_ref, keys, values, queries, z_keys, z_values) = rest[:-6], rest[-6:]
    me, x_at = at_ref[0], at_ref[1]
    upper = me >= 2
    length = low_own.shape[2]
    below, above = slice(0, length), slice(length, 2 * length)
    gather_queries(me, queries, (got0, got1, got2, got3))
    for which, store in ((0, keys), (1, values)):
        for slot in range(2):
            at = 1 + (me ^ slot)
            store[at, below] = jnp.where(x_at == 0, second[slot, which], low_own[slot, which])
            store[at, above] = jnp.where(
                x_at == XN - 1, second[slot, which], high_own[slot, which]
            )
            at = 1 + (me ^ slot ^ 2)
            store[at, below] = jnp.where(x_at == 0, direct[slot, which], low_oth[slot, which])
            store[at, above] = jnp.where(x_at == XN - 1, direct[slot, which], high_oth[slot, which])
        z_store = z_keys if which == 0 else z_values
        for slot in range(2):
            at = me ^ slot
            z_store[jnp.where(upper, at - 2, at + 2)] = z_own[slot, which]
            at = at ^ 2
            z_store[jnp.where(upper, at + 2, at - 2)] = z_oth[slot, which]
        for arrived, at in zip(corners, (jnp.where(upper, 0, 5), jnp.where(upper, 5, 0))):
            store[at, length - BLK : length + BLK] = arrived[which]
    reaches = [(step, (REACH - abs(step)) * BLK) for step in HALO_STEPS]
    units = [
        (at, frame, slice(head * HDIM, (head + 1) * HDIM))
        for head in range(low_own.shape[3] // HDIM)
        for at, frame in enumerate(frames)
    ]

    z_frames = (-2, -1, GROUP, GROUP + 1)
    z_near = [[z for z in z_frames if abs(z - frame) <= REACH] for frame in range(GROUP)]

    def spans(store, z_store, frame, lanes):
        return [z_store[z_frames.index(z), :, lanes] for z in z_near[frame]] + [
            store[frame + 1 + step, length - reach : length + reach, lanes]
            for step, reach in reaches
        ]

    biases = {
        frame: jnp.concatenate(
            [own_bias(bias_ref, frame, z_near[frame]), bias_ref[frame, :, OWN_KEYS:]], axis=1
        )
        for frame in frames
    }
    scores = [
        head_scores(queries[frame, :, lanes], spans(keys, z_keys, frame, lanes), biases[frame])
        for _, frame, lanes in units
    ]
    tops = [
        jnp.maximum(top_in[frame, :, lanes], jnp.max(s, axis=1, keepdims=True))
        for s, (_, frame, lanes) in zip(scores, units)
    ]
    weights = [jnp.exp2((s - top[:, 0:1]) * SCALE) for s, top in zip(scores, tops)]
    totals = [jnp.sum(w, axis=1, keepdims=True) for w in weights]
    for top, w, total, (at, frame, lanes) in zip(tops, weights, totals, units):
        again = jnp.exp2((top_in[frame, :, lanes] - top) * SCALE)
        out = sofar[frame, :, lanes] * again + weighted(
            w, spans(values, z_values, frame, lanes)
        )
        total = sum_in[frame, :, lanes] * again + total
        out_ref[at, :, lanes] = (out / total).astype(jnp.bfloat16)


def attend(kernel, out_shape, scratches, work, place, bias, arrays, after=()):
    length, width = arrays[0].shape[1:]
    return pl.pallas_call(
        kernel,
        in_specs=[SMEM] + [VMEM] * (1 + len(arrays)) + [ANY] * len(after),
        out_specs=jax.tree.map(lambda _: VMEM, out_shape),
        out_shape=out_shape,
        scratch_shapes=[pltpu.VMEM(scratch, jnp.bfloat16) for scratch in scratches],
        compiler_params=pltpu.CompilerParams(vmem_limit_bytes=24 * 2**20),
        cost_estimate=pl.CostEstimate(
            flops=4 * work * width * length, bytes_accessed=8_000_000,
            transcendentals=work * width * length // HDIM,
        ),
    )(place, bias, *arrays, *after)


def shards(frame_total, row_total, queries, key_states, value_states, radial_mask):
    length, width = queries.shape[1:]
    part = width // GROUP
    frame_at = lax.axis_index("frame")
    row_at = lax.axis_index("row")
    me = frame_at % GROUP
    x_at = row_at % XN
    place = jnp.stack([me, x_at]).astype(jnp.int32)

    def send(array, target):
        return lax.ppermute(array, AXES, pairs_of(frame_total, row_total, target))

    packed = pl.pallas_call(
        pack_kernel,
        in_specs=[ANY] * 3,
        out_specs=[VMEM] * GROUP,
        out_shape=[jax.ShapeDtypeStruct((3, length, part), jnp.bfloat16)] * GROUP,
        scratch_shapes=[pltpu.SemaphoreType.DMA((GROUP, 3))],
        compiler_params=pltpu.CompilerParams(vmem_limit_bytes=56 * 2**20),
    )(queries[0], key_states[0], value_states[0])

    def flip(bits):
        return lambda f, r: (f ^ bits, r)

    groups = [list(range(f, f + GROUP)) for f in range(0, frame_total, GROUP)]
    arrived = [packed[0]] + [send(packed[s], flip(s)) for s in range(1, GROUP)]
    own = join(arrived[0], arrived[1])

    def row_first(by):
        edge = XN - 1 if by > 0 else 0
        return lambda f, r: (f, r + by) if r % XN != edge else (f, r - by * (XN - 1))

    def row_second(f, r):
        return (f, r + XN) if r % XN == 0 else (f, r - XN) if r % XN == XN - 1 else None

    def row_inner(by):
        edge = XN - 1 if by > 0 else 0
        return lambda f, r: (f, r + by) if r % XN != edge else None

    def row_across(f, r):
        return (f, r + 1) if r % XN == XN - 1 else (f, r - 1) if r % XN == 0 else None

    def z_target(own_pair):
        def target(f, r):
            up = (f % GROUP >= 2) == own_pair
            return (f + GROUP if up else f - GROUP, r)

        return target

    low_own, high_own = send(own, row_first(1)), send(own, row_first(-1))
    z_own = send(own, z_target(True))
    oth = join(arrived[2], arrived[3])
    direct = send(oth, row_across)
    wrapped = wrapped_of(place, low_own, high_own, oth)
    second = send(wrapped, row_second)

    bias = bias_of(radial_mask, frame_at - me, row_at, frame_total)
    sums = [jax.ShapeDtypeStruct((GROUP, length, part), jnp.float32)] * 3
    partial = attend(
        own_kernel, sums, [(GROUP, length, part)] * 3, 14 * length, place, bias,
        arrived + [own, oth], [wrapped, z_own],
    )
    later = join(arrived[2], arrived[3], partial[0])
    low_oth, high_oth = send(later, row_inner(1)), send(later, row_inner(-1))
    z_oth = send(later, z_target(False))
    c_own, c_oth = corners_of(place, low_own, high_own, second, low_oth, high_oth, direct)
    c_own, c_oth = send(c_own, z_target(True)), send(c_oth, z_target(False))

    arrays = arrived + list(partial) + [low_own, high_own, second, low_oth, high_oth, direct]
    arrays += [z_own, z_oth]
    group_shape = (GROUP, length, part)
    half = jax.ShapeDtypeStruct((2, length, part), jnp.bfloat16)
    halo_keys = bias.shape[2] - OWN_KEYS
    middle, edge = [
        attend(
            functools.partial(halo_kernel, frames), half,
            [(GROUP + 2, 2 * length, part)] * 2 + [group_shape] * 3, 2 * halo_keys, place, bias, arrays + corners,
        )
        for frames, corners in (((1, 2), []), ((0, 3), [c_own, c_oth]))
    ]
    by_frame = jnp.stack([edge[0], middle[0], middle[1], edge[1]])
    back = lax.all_to_all(by_frame, "frame", 0, 0, axis_index_groups=groups)
    result = pl.pallas_call(
        unpack_kernel,
        in_specs=[ANY],
        out_specs=ANY,
        out_shape=jax.ShapeDtypeStruct((length, width), jnp.bfloat16),
        scratch_shapes=[pltpu.SemaphoreType.DMA((GROUP,))],
        compiler_params=pltpu.CompilerParams(vmem_limit_bytes=4 * 2**20),
    )(back)
    return result[None]


def solution(mesh):
    sharded = P("frame", "row", None)
    body = functools.partial(shards, mesh.shape["frame"], mesh.shape["row"])
    return jax.shard_map(
        body, mesh=mesh, in_specs=(sharded, sharded, sharded, P()), out_specs=sharded, check_vma=False
    )
```

```python
import functools

import jax
import jax.numpy as jnp
import numpy as np
from jax import lax
from jax.experimental import pallas as pl
from jax.experimental.pallas import tpu as pltpu
from jax.sharding import PartitionSpec as P

HDIM = 128
BLK = 64
REACH = 2
NEG = -1e30
SCALE = HDIM ** -0.5 * 1.4426950408889634
AXES = ("frame", "row")
GROUP = 4
XN = 4
VMEM = pl.BlockSpec(memory_space=pltpu.VMEM)
SMEM = pl.BlockSpec(memory_space=pltpu.SMEM)
ANY = pl.BlockSpec(memory_space=pl.ANY)
FRAME_STEPS = (-2, -1, 0, 1, 2)
HALO_STEPS = (-1, 0, 1)
OWN_KEYS = 2 * BLK * len(FRAME_STEPS)


def pairs_of(frames, rows, target):
    pairs = []
    for frame in range(frames):
        for row in range(rows):
            to = target(frame, row)
            if to is not None and 0 <= to[0] < frames and 0 <= to[1] < rows:
                pairs.append((frame * rows + row, to[0] * rows + to[1]))
    return pairs


def key_block_table():
    own = [(step, block) for step in FRAME_STEPS for block in (0, 1)]
    halo = []
    for step in HALO_STEPS:
        reach = REACH - abs(step)
        halo += [(step, block) for block in range(-reach, 0)]
        halo += [(step, block) for block in range(2, 2 + reach)]
    return own + halo


def bias_of(radial_mask, frame_first, row_at, frame_total):
    table = key_block_table()
    offsets = 2 * REACH + 1
    pick = np.zeros((2, len(table), offsets * 2 * offsets), np.float32)
    for query in range(2):
        for at, (step, block) in enumerate(table):
            offset = block - query + REACH
            if 0 <= offset < offsets:
                pick[query, at, ((step + REACH) * 2 + query) * offsets + offset] = 1.0
    rows = lax.dynamic_slice_in_dim(radial_mask, row_at * 2, 2, 1)
    chosen = jnp.sum(jnp.asarray(pick) * rows.reshape(1, 1, -1).astype(jnp.float32), axis=2)
    steps = jnp.asarray(np.array([s for s, _ in table], np.int32))
    blocks = jnp.asarray(np.array([b for _, b in table], np.int32)) + row_at * 2
    inside = (blocks >= 0) & (blocks < radial_mask.shape[1])
    frames = frame_first + jnp.arange(GROUP, dtype=jnp.int32)[:, None] + steps[None, :]
    valid = (frames >= 0) & (frames < frame_total) & inside[None, :]
    allowed = (chosen[None] > 0) & valid[:, None, :]
    bias = jnp.where(allowed, 0.0, NEG).astype(jnp.float32)
    return jnp.repeat(bias, BLK, axis=2)


def pack_kernel(q_ref, k_ref, v_ref, out0, out1, out2, out3, sems):
    me = lax.axis_index("frame") % GROUP
    outs = (out0, out1, out2, out3)
    width = out0.shape[2]
    copies = []
    for slot in (1, 2, 3, 0):
        columns = pl.ds(pl.multiple_of((me ^ slot) * width, HDIM), width)
        for which, source in enumerate((k_ref, v_ref, q_ref)):
            copies.append(
                pltpu.make_async_copy(
                    source.at[:, columns], outs[slot].at[which], sems.at[slot, which]
                )
            )
    for copy in copies:
        copy.start()
    for copy in copies:
        copy.wait()


def unpack_kernel(in_ref, out_ref, sems):
    width = in_ref.shape[2]
    copies = [
        pltpu.make_async_copy(
            in_ref.at[part], out_ref.at[:, pl.ds(part * width, width)], sems.at[part]
        )
        for part in range(GROUP)
    ]
    for copy in copies:
        copy.start()
    for copy in copies:
        copy.wait()


def join_kernel(first, second, *rest):
    out, sems = rest[-2:]
    copies = [
        pltpu.make_async_copy(source.at[0:2], out.at[slot], sems.at[slot])
        for slot, source in enumerate((first, second))
    ]
    for copy in copies:
        copy.start()
    for copy in copies:
        copy.wait()


def join(first, second, *after):
    return pl.pallas_call(
        join_kernel,
        in_specs=[ANY] * (2 + len(after)),
        out_specs=VMEM,
        out_shape=jax.ShapeDtypeStruct((2, 2) + first.shape[1:], jnp.bfloat16),
        scratch_shapes=[pltpu.SemaphoreType.DMA((2,))],
        compiler_params=pltpu.CompilerParams(vmem_limit_bytes=4 * 2**20),
    )(first, second, *after)


def wrapped_kernel(at_ref, low, high, after, out, sem):
    del after
    x_at = at_ref[1]

    @pl.when(x_at == 0)
    def _():
        pltpu.make_async_copy(low, out, sem).start()

    @pl.when(x_at != 0)
    def _():
        pltpu.make_async_copy(high, out, sem).start()

    pltpu.make_async_copy(low, out, sem).wait()


def wrapped_of(place, low, high, after):
    return pl.pallas_call(
        wrapped_kernel,
        in_specs=[SMEM] + [ANY] * 3,
        out_specs=VMEM,
        out_shape=jax.ShapeDtypeStruct(low.shape, jnp.bfloat16),
        scratch_shapes=[pltpu.SemaphoreType.DMA(())],
        compiler_params=pltpu.CompilerParams(vmem_limit_bytes=4 * 2**20),
    )(place, low, high, after)


def corner_kernel(
    at_ref, low_own, high_own, second, low_oth, high_oth, direct, out_own, out_oth, sems
):
    me, x_at = at_ref[0], at_ref[1]
    length = low_own.shape[2]
    own = (jnp.where(me < 2, me, 3 - me), out_own, 0)
    oth = (jnp.where(me < 2, 1 - me, me - 2), out_oth, 2)

    def from_low(source, slot, out, sem):
        rows = pl.ds(length - BLK, BLK)
        return pltpu.make_async_copy(source.at[slot, :, rows], out.at[:, pl.ds(0, BLK)], sems.at[sem])

    def from_high(source, slot, out, sem):
        rows = pl.ds(0, BLK)
        return pltpu.make_async_copy(
            source.at[slot, :, rows], out.at[:, pl.ds(BLK, BLK)], sems.at[sem + 1]
        )

    @pl.when(x_at == 0)
    def _():
        from_low(second, *own).start()
        from_low(direct, *oth).start()

    @pl.when(x_at != 0)
    def _():
        from_low(low_own, *own).start()
        from_low(low_oth, *oth).start()

    @pl.when(x_at == XN - 1)
    def _():
        from_high(second, *own).start()
        from_high(direct, *oth).start()

    @pl.when(x_at != XN - 1)
    def _():
        from_high(high_own, *own).start()
        from_high(high_oth, *oth).start()

    from_low(low_own, *own).wait()
    from_high(high_own, *own).wait()
    from_low(low_oth, *oth).wait()
    from_high(high_oth, *oth).wait()


def corners_of(place, *arrays):
    shape = jax.ShapeDtypeStruct((2, 2 * BLK, arrays[0].shape[3]), jnp.bfloat16)
    return pl.pallas_call(
        corner_kernel,
        in_specs=[SMEM] + [ANY] * len(arrays),
        out_specs=[VMEM] * 2,
        out_shape=[shape] * 2,
        scratch_shapes=[pltpu.SemaphoreType.DMA((4,))],
        compiler_params=pltpu.CompilerParams(vmem_limit_bytes=4 * 2**20),
    )(place, *arrays)


def head_scores(query, keys, bias):
    scores = jnp.concatenate(
        [
            lax.dot_general(query, k, (((1,), (1,)), ((), ())), preferred_element_type=jnp.float32)
            for k in keys
        ],
        axis=1,
    )
    return jnp.concatenate([scores[:BLK] + bias[0:1], scores[BLK:] + bias[1:2]], axis=0)


def own_bias(bias_ref, frame, near):
    start = (near[0] - frame + REACH) * 2 * BLK
    return bias_ref[frame, :, start : start + len(near) * 2 * BLK]


def weighted(weights, values):
    rounded = weights.astype(jnp.bfloat16)
    start, out = 0, 0
    for v in values:
        out = out + jnp.dot(
            rounded[:, start : start + v.shape[0]], v, preferred_element_type=jnp.float32
        )
        start += v.shape[0]
    return out


def gather_queries(me, queries, got):
    for slot, array in enumerate(got):
        queries[me ^ slot] = array[2]


def own_kernel(
    at_ref, bias_ref, got0, got1, got2, got3, own, oth, after0, after1, out_ref, top_ref, sum_ref, keys, values, queries,
):
    del after0, after1
    me = at_ref[0]
    gather_queries(me, queries, (got0, got1, got2, got3))
    for which, store in ((0, keys), (1, values)):
        for slot in range(2):
            store[me ^ slot] = own[slot, which]
            store[me ^ slot ^ 2] = oth[slot, which]
    near = [range(max(frame - REACH, 0), min(frame + REACH + 1, GROUP)) for frame in range(GROUP)]
    for head in range(own.shape[3] // HDIM):
        lanes = slice(head * HDIM, (head + 1) * HDIM)
        scores = [
            head_scores(
                queries[frame, :, lanes],
                [keys[at, :, lanes] for at in near[frame]],
                own_bias(bias_ref, frame, near[frame]),
            )
            for frame in range(GROUP)
        ]
        tops = [jnp.max(s, axis=1, keepdims=True) for s in scores]
        weights = [jnp.exp2((s - top) * SCALE) for s, top in zip(scores, tops)]
        totals = [jnp.sum(w, axis=1, keepdims=True) for w in weights]
        for frame in range(GROUP):
            out_ref[frame, :, lanes] = weighted(
                weights[frame], [values[at, :, lanes] for at in near[frame]]
            )
            shape = (tops[frame].shape[0], HDIM)
            top_ref[frame, :, lanes] = jnp.broadcast_to(tops[frame], shape)
            sum_ref[frame, :, lanes] = jnp.broadcast_to(totals[frame], shape)


def halo_kernel(
    frames, at_ref, bias_ref, got0, got1, got2, got3, sofar, top_in, sum_in,
    low_own, high_own, second, low_oth, high_oth, direct, z_own, z_oth, *rest
):
    corners, (out_ref, keys, values, queries, z_keys, z_values) = rest[:-6], rest[-6:]
    me, x_at = at_ref[0], at_ref[1]
    upper = me >= 2
    length = low_own.shape[2]
    below, above = slice(0, length), slice(length, 2 * length)
    gather_queries(me, queries, (got0, got1, got2, got3))
    for which, store in ((0, keys), (1, values)):
        for slot in range(2):
            at = 1 + (me ^ slot)
            store[at, below] = jnp.where(x_at == 0, second[slot, which], low_own[slot, which])
            store[at, above] = jnp.where(
                x_at == XN - 1, second[slot, which], high_own[slot, which]
            )
            at = 1 + (me ^ slot ^ 2)
            store[at, below] = jnp.where(x_at == 0, direct[slot, which], low_oth[slot, which])
            store[at, above] = jnp.where(x_at == XN - 1, direct[slot, which], high_oth[slot, which])
        z_store = z_keys if which == 0 else z_values
        for slot in range(2):
            at = me ^ slot
            z_store[jnp.where(upper, at - 2, at + 2)] = z_own[slot, which]
            at = at ^ 2
            z_store[jnp.where(upper, at + 2, at - 2)] = z_oth[slot, which]
        for arrived, at in zip(corners, (jnp.where(upper, 0, 5), jnp.where(upper, 5, 0))):
            store[at, length - BLK : length + BLK] = arrived[which]
    reaches = [(step, (REACH - abs(step)) * BLK) for step in HALO_STEPS]
    units = [
        (at, frame, slice(head * HDIM, (head + 1) * HDIM))
        for head in range(low_own.shape[3] // HDIM)
        for at, frame in enumerate(frames)
    ]

    z_frames = (-2, -1, GROUP, GROUP + 1)
    z_near = [[z for z in z_frames if abs(z - frame) <= REACH] for frame in range(GROUP)]

    def spans(store, z_store, frame, lanes):
        return [z_store[z_frames.index(z), :, lanes] for z in z_near[frame]] + [
            store[frame + 1 + step, length - reach : length + reach, lanes]
            for step, reach in reaches
        ]

    biases = {
        frame: jnp.concatenate(
            [own_bias(bias_ref, frame, z_near[frame]), bias_ref[frame, :, OWN_KEYS:]], axis=1
        )
        for frame in frames
    }
    scores = [
        head_scores(queries[frame, :, lanes], spans(keys, z_keys, frame, lanes), biases[frame])
        for _, frame, lanes in units
    ]
    tops = [
        jnp.maximum(top_in[frame, :, lanes], jnp.max(s, axis=1, keepdims=True))
        for s, (_, frame, lanes) in zip(scores, units)
    ]
    weights = [jnp.exp2((s - top[:, 0:1]) * SCALE) for s, top in zip(scores, tops)]
    totals = [jnp.sum(w, axis=1, keepdims=True) for w in weights]
    for top, w, total, (at, frame, lanes) in zip(tops, weights, totals, units):
        again = jnp.exp2((top_in[frame, :, lanes] - top) * SCALE)
        out = sofar[frame, :, lanes] * again + weighted(
            w, spans(values, z_values, frame, lanes)
        )
        total = sum_in[frame, :, lanes] * again + total
        out_ref[at, :, lanes] = (out / total).astype(jnp.bfloat16)


def attend(kernel, out_shape, scratches, work, place, bias, arrays, after=()):
    length, width = arrays[0].shape[1:]
    return pl.pallas_call(
        kernel,
        in_specs=[SMEM] + [VMEM] * (1 + len(arrays)) + [ANY] * len(after),
        out_specs=jax.tree.map(lambda _: VMEM, out_shape),
        out_shape=out_shape,
        scratch_shapes=[pltpu.VMEM(scratch, jnp.bfloat16) for scratch in scratches],
        compiler_params=pltpu.CompilerParams(vmem_limit_bytes=18 * 2**20),
        cost_estimate=pl.CostEstimate(
            flops=4 * work * width * length, bytes_accessed=8_000_000,
            transcendentals=work * width * length // HDIM,
        ),
    )(place, bias, *arrays, *after)


def shards(frame_total, row_total, queries, key_states, value_states, radial_mask):
    length, width = queries.shape[1:]
    part = width // GROUP
    frame_at = lax.axis_index("frame")
    row_at = lax.axis_index("row")
    me = frame_at % GROUP
    x_at = row_at % XN
    place = jnp.stack([me, x_at]).astype(jnp.int32)

    def send(array, target):
        return lax.ppermute(array, AXES, pairs_of(frame_total, row_total, target))

    packed = pl.pallas_call(
        pack_kernel,
        in_specs=[ANY] * 3,
        out_specs=[VMEM] * GROUP,
        out_shape=[jax.ShapeDtypeStruct((3, length, part), jnp.bfloat16)] * GROUP,
        scratch_shapes=[pltpu.SemaphoreType.DMA((GROUP, 3))],
        compiler_params=pltpu.CompilerParams(vmem_limit_bytes=56 * 2**20),
    )(queries[0], key_states[0], value_states[0])

    def flip(bits):
        return lambda f, r: (f ^ bits, r)

    groups = [list(range(f, f + GROUP)) for f in range(0, frame_total, GROUP)]
    arrived = [packed[0]] + [send(packed[s], flip(s)) for s in range(1, GROUP)]
    own = jnp.stack([arrived[0][:2], arrived[1][:2]])

    def row_first(by):
        edge = XN - 1 if by > 0 else 0
        return lambda f, r: (f, r + by) if r % XN != edge else (f, r - by * (XN - 1))

    def row_second(f, r):
        return (f, r + XN) if r % XN == 0 else (f, r - XN) if r % XN == XN - 1 else None

    def row_inner(by):
        edge = XN - 1 if by > 0 else 0
        return lambda f, r: (f, r + by) if r % XN != edge else None

    def row_across(f, r):
        return (f, r + 1) if r % XN == XN - 1 else (f, r - 1) if r % XN == 0 else None

    def z_target(own_pair):
        def target(f, r):
            up = (f % GROUP >= 2) == own_pair
            return (f + GROUP if up else f - GROUP, r)

        return target

    low_own, high_own = send(own, row_first(1)), send(own, row_first(-1))
    z_own = send(own, z_target(True))
    oth = join(arrived[2], arrived[3])
    direct = send(oth, row_across)
    wrapped = wrapped_of(place, low_own, high_own, oth)
    second = send(wrapped, row_second)

    bias = bias_of(radial_mask, frame_at - me, row_at, frame_total)
    sums = [jax.ShapeDtypeStruct((GROUP, length, part), jnp.float32)] * 3
    partial = attend(
        own_kernel, sums, [(GROUP, length, part)] * 3, 14 * length, place, bias,
        arrived + [own, oth], [wrapped, z_own],
    )
    later = join(arrived[2], arrived[3], partial[0])
    low_oth, high_oth = send(later, row_inner(1)), send(later, row_inner(-1))
    z_oth = send(later, z_target(False))
    c_own, c_oth = corners_of(place, low_own, high_own, second, low_oth, high_oth, direct)
    c_own, c_oth = send(c_own, z_target(True)), send(c_oth, z_target(False))

    arrays = arrived + list(partial) + [low_own, high_own, second, low_oth, high_oth, direct]
    arrays += [z_own, z_oth]
    group_shape = (GROUP, length, part)
    half = jax.ShapeDtypeStruct((2, length, part), jnp.bfloat16)
    halo_keys = bias.shape[2] - OWN_KEYS
    middle, edge = [
        attend(
            functools.partial(halo_kernel, frames), half,
            [(GROUP + 2, 2 * length, part)] * 2 + [group_shape] * 3, 2 * halo_keys, place, bias, arrays + corners,
        )
        for frames, corners in (((1, 2), []), ((0, 3), [c_own, c_oth]))
    ]
    by_frame = jnp.stack([edge[0], middle[0], middle[1], edge[1]])
    back = lax.all_to_all(by_frame, "frame", 0, 0, axis_index_groups=groups)
    result = pl.pallas_call(
        unpack_kernel,
        in_specs=[ANY],
        out_specs=ANY,
        out_shape=jax.ShapeDtypeStruct((length, width), jnp.bfloat16),
        scratch_shapes=[pltpu.SemaphoreType.DMA((GROUP,))],
        compiler_params=pltpu.CompilerParams(vmem_limit_bytes=4 * 2**20),
    )(back)
    return result[None]


def solution(mesh):
    sharded = P("frame", "row", None)
    body = functools.partial(shards, mesh.shape["frame"], mesh.shape["row"])
    return jax.shard_map(
        body, mesh=mesh, in_specs=(sharded, sharded, sharded, P()), out_specs=sharded, check_vma=False
    )
```
